512 devices in a mesh: replica: 8 (over z_hi, core), fsdp: 64 (over y, z_lo, x).
Axes of the slice: x: 4, y: 4, z: 16 (z_hi: 4, z_lo: 4; z = z_hi * 4 + z_lo), core: 2. Of those that a mesh axis runs over, the one named last changes fastest.
Arguments:
- inputs: bfloat16 [12288, 8192], P('fsdp'), may hold values from -6 to 6
- local_weights: float32 [8, 512, 8192], P('replica', 'fsdp'), may hold values from -8 to 8
- global_base: float32 [512, 8192], P('fsdp'), may hold values from -4 to 4
- momentum: float32 [512, 8192], P('fsdp'), may hold values from -3 to 3
Outputs:
- new_base: float32 [512, 8192], P('fsdp')
- new_momentum: float32 [512, 8192], P('fsdp')
- keys: bfloat16 [12288, 512], P('fsdp')
The draws below stay inside these ranges and needn't reach their ends.
All inputs are finite; a program needn't handle non-finite values.
Results may differ from the reference program's by a relative error of at most 0.014.
Values may be sent and summed in bfloat16 or wider, within the bound.
A program may use at most 64 MiB of HBM per device.

```python
import jax
import jax.numpy as jnp
from jax import lax

D = 8192
QBLOCK = 128
TOKENS = 12288
FRAG_ROWS = 512
REPLICAS = 8


def shared_base(key):
    field = jax.random.normal(jax.random.fold_in(key, 5), (FRAG_ROWS, D), jnp.float32)
    return jnp.clip(field, -4.0, 4.0)


def draw_global_base(key, part):
    return shared_base(key)


def draw_local_weights(key, part):
    anchor = shared_base(key)
    key = jax.random.fold_in(key, 7)
    subkeys = jax.random.split(key, 10)
    full_shape = (REPLICAS, FRAG_ROWS, D // QBLOCK, QBLOCK)
    head_shape = (REPLICAS, FRAG_ROWS, D // QBLOCK, 1)
    exponent = jax.random.randint(subkeys[0], head_shape, 5, 9)
    peak_level = jax.random.randint(subkeys[1], head_shape, 65, 121)
    lowest = peak_level // 4
    bound_level = lowest + jax.random.randint(subkeys[2], head_shape, 0, 1 << 20) % (peak_level - lowest)
    spread = 2 * bound_level + 1
    levels = jax.random.randint(subkeys[3], full_shape, 0, 1 << 20) % spread - bound_level
    fraction = jax.random.uniform(subkeys[6], full_shape, jnp.float32, -0.35, 0.35)
    peak_slot = jax.random.randint(subkeys[7], head_shape, 0, QBLOCK)
    peak_frac = jax.random.uniform(subkeys[8], head_shape, jnp.float32, -0.35, 0.0)
    peak_sign = (jax.random.randint(subkeys[9], head_shape, 0, 2) * 2 - 1).astype(jnp.float32)
    column = lax.broadcasted_iota(jnp.int32, full_shape, 3)
    entries = jnp.where(column == peak_slot, peak_sign * (peak_level.astype(jnp.float32) + peak_frac), levels.astype(jnp.float32) + fraction)
    divisor = jnp.left_shift(jnp.ones_like(exponent), exponent).astype(jnp.float32)
    pseudo_grad = (entries / divisor).reshape(REPLICAS, FRAG_ROWS, D)
    return anchor[None] - pseudo_grad


def shard_levels(own_key, dims, cuts, smallest, largest):
    level, own = 1.0, jax.random.fold_in(own_key, 6)
    for position, shards_of in cuts:
        draws = jnp.exp(jax.random.uniform(jax.random.fold_in(own, position), (shards_of,), jnp.float32, smallest / len(cuts), largest / len(cuts)))
        level = level * jnp.repeat(draws, dims[position] // shards_of).reshape([-1 if axis == position else 1 for axis in range(len(dims))])
    return level


def scatter_about(own_key, shape, deviation, bound, shards=(), kind=jnp.bfloat16):
    values = deviation * jax.random.normal(own_key, shape, jnp.float32)
    if shards:
        values = values * shard_levels(own_key, shape, shards, -0.22, 0.18)
    return jnp.clip(values, -bound, bound).astype(kind)


def setup_inputs(seed: int = 0) -> dict:
    splits = jax.random.split(jax.random.key(seed), 5)
    return {
        "inputs": scatter_about(splits[0], (TOKENS, D), 1.0, 6.0, ((0, 64),)),
        "local_weights": draw_local_weights(jax.random.fold_in(splits[4], 71), 0),
        "global_base": draw_global_base(jax.random.fold_in(splits[4], 71), 0),
        "momentum": scatter_about(splits[3], (FRAG_ROWS, D), 0.5, 3.0, ((0, 64),), jnp.float32),
    }


EPSILON = 1e-6
CODE_RANGE = 127.0
OUTER_RATE = 0.7
OUTER_MOMENTUM = 0.9


def reference(inputs, local_weights, global_base, momentum):
    pseudo_grad = global_base[None] - local_weights
    blocks = pseudo_grad.reshape(REPLICAS, FRAG_ROWS, D // QBLOCK, QBLOCK)
    block_max = jnp.max(jnp.abs(blocks), axis=-1)
    block_scale = jnp.exp2(jnp.ceil(jnp.log2((block_max + EPSILON) / CODE_RANGE))).astype(jnp.bfloat16)
    quant_codes = jnp.floor(blocks / block_scale.astype(jnp.float32)[..., None] + 0.5).astype(jnp.bfloat16)
    restored = quant_codes.astype(jnp.float32) * block_scale.astype(jnp.float32)[..., None]
    outer_grad = jnp.sum(restored, axis=0).reshape(FRAG_ROWS, D) / REPLICAS
    new_momentum = OUTER_MOMENTUM * momentum + outer_grad
    new_base = global_base - OUTER_RATE * (outer_grad + OUTER_MOMENTUM * new_momentum)
    weight = new_base.astype(jnp.bfloat16)
    keys = jnp.dot(inputs, weight.T, preferred_element_type=jnp.float32).astype(jnp.bfloat16)
    return new_base, new_momentum, keys
```

```python
import jax
import jax.numpy as jnp
from jax import lax
from jax.experimental import pallas as pl
from jax.experimental.pallas import tpu as pltpu
from jax.sharding import PartitionSpec as P

MESH = pl.DeviceIdType.MESH
F32, BF16 = jnp.float32, jnp.bfloat16
EPSILON = 1e-06
CODE_RANGE = 127.0
OUTER_RATE = 0.7
OUTER_MOMENTUM = 0.9
QBLOCK = 128
BLOCKS = 64
ROWS = 8
HALF = 32
SLOTS = 64
TOKENS = 192
PACKED = TOKENS // 2


def rem(a, b):
    return lax.rem(a, jnp.int32(b))


def div(a, b):
    return lax.div(a, jnp.int32(b))


def device(z, core, y, x):
    return (2 * div(z, 4) + core, 16 * y + 4 * rem(z, 4) + x)


def parity(x, y):
    return 1 - 2 * rem(x + y, 2)


def rows(start, count):
    return pl.ds(pl.multiple_of(start, count), count)


def kernel(
    inp, lw, base, mom, nb_out, nm_out, keys_out,
    lw_v, base_v, mom_v, x_v, spread, core_send, core_recv, far_send, far_recv, lead_send, lead_recv,
    pieces, turned, weight, og_own, og_recv, og_other, part, perm, keys_v,
    load_sem, core_sem, far_ssem, far_rsem, lead_sem, piece_ssem, piece_rsem, og_ssem, og_rsem, ogc_sem,
    key_ssem, key_rsem, out_sem,
):
    replica = lax.axis_index("replica")
    fsdp = lax.axis_index("fsdp")
    z_hi, core = div(replica, 2), rem(replica, 2)
    y, z_lo, x = div(fsdp, 16), rem(div(fsdp, 4), 4), rem(fsdp, 4)
    z = 4 * z_hi + z_lo
    mine = parity(x, y)

    def at(dz=0, dy=0, dx=0, other=False):
        return device(
            rem(z + dz + 16, 16), 1 - core if other else core, rem(y + dy, 4), rem(x + dx, 4)
        )

    def remote(src, dst, ssem, rsem, to):
        return pltpu.make_async_remote_copy(
            src_ref=src, dst_ref=dst, send_sem=ssem, recv_sem=rsem, device_id=to, device_id_type=MESH
        )

    loads = [
        pltpu.make_async_copy(lw, lw_v, load_sem.at[0]),
        pltpu.make_async_copy(base, base_v, load_sem.at[1]),
        pltpu.make_async_copy(mom, mom_v, load_sem.at[2]),
        pltpu.make_async_copy(inp, x_v, load_sem.at[3]),
    ]
    for load in loads:
        load.start()

    barrier = pltpu.get_barrier_semaphore()
    greeted = 0

    def greet(to):
        pl.semaphore_signal(barrier, inc=1, device_id=to, device_id_type=MESH)

    for dz in (6, -6, 2, -2):
        greet(at(dz))
        greeted += 1
    for dx in range(4):
        there = parity(rem(x + dx, 4), y)
        for dz in (0, 1, -1, None):
            if dx or dz != 0:
                greet(at(-2 * there if dz is None else -dz, 0, dx))
                greeted += 1
    for dy in range(1, 4):
        there = parity(x, rem(y + dy, 4))
        for dz in (0, 1, -1, None):
            greet(at(-2 * there if dz is None else -dz, dy))
            greeted += 1
    greet(at(other=True))
    greeted += 1

    loads[0].wait()
    loads[1].wait()

    def quantize(step, carry):
        for k in range(4):
            b = step * 4 + k
            columns = rows(b * QBLOCK, QBLOCK)
            pseudo = base_v[:, columns] - lw_v[:, columns]
            peak = jnp.max(jnp.abs(pseudo), axis=-1, keepdims=True)
            scale = jnp.exp2(jnp.ceil(jnp.log2((peak + EPSILON) / CODE_RANGE)))
            scale = scale.astype(BF16).astype(F32)
            codes = jnp.floor(pseudo / scale + 0.5).astype(BF16).astype(F32)
            spread[rows(b * ROWS, ROWS), :] = codes * scale
        return carry

    lax.fori_loop(0, BLOCKS // 4, quantize, 0)

    def row(ref, q):
        return ref[pl.ds(q, BLOCKS, stride=ROWS), :]

    for k in range(4):
        core_send[k * BLOCKS : (k + 1) * BLOCKS, :] = row(spread, 2 * k + 1 - core).astype(BF16)

    pl.semaphore_wait(barrier, greeted)

    swap = remote(core_send, core_recv, core_sem.at[0], core_sem.at[1], at(other=True))
    swap.start()

    loads[2].wait()
    lead_q = 2 * div(rem(z + 2, 16), 4) + core
    keep = [row(spread, 2 * k + core) for k in range(4)]

    def lead_rows(step, carry):
        for k in range(4):
            b = step * 4 + k
            columns = rows(b * QBLOCK, QBLOCK)
            turned[rows(b * ROWS, ROWS), :] = base_v[:, columns] - (
                OUTER_RATE * OUTER_MOMENTUM * OUTER_MOMENTUM
            ) * mom_v[:, columns]
        return carry

    lax.fori_loop(0, BLOCKS // 4, lead_rows, 0)
    lead_send[...] = row(turned, lead_q)

    swap.wait_recv()
    for k in range(4):
        part_sum = keep[k] + core_recv[k * BLOCKS : (k + 1) * BLOCKS, :].astype(F32)
        far_send[k * BLOCKS : (k + 1) * BLOCKS, :] = part_sum.astype(BF16)
    fars = []
    for j, dz in enumerate((6, -6, 2, -2)):
        k = div(rem(z + dz + 16, 16), 4)
        fars.append(
            remote(
                far_send.at[rows(k * BLOCKS, BLOCKS)],
                far_recv.at[pl.ds(j * BLOCKS, BLOCKS)],
                far_ssem.at[j],
                far_rsem.at[j],
                at(dz),
            )
        )
        fars[-1].start()
    lead = remote(lead_send, lead_recv, lead_sem.at[0], lead_sem.at[1], at(2))
    lead.start()

    def order(j, carry):
        late = jnp.where(j >= 6, 1, 0)
        other = late * (j - 6) + (1 - late) * div(j, 3)
        turn = late * 2 + (1 - late) * rem(j * j, 3) * (1 + 2 * jnp.where(rem(j, 3) == 2, 1, 0))
        there_hi = z_hi + turn
        there_core = rem(core + other, 2)
        line = lax.broadcasted_iota(jnp.int32, (128, QBLOCK), 0)
        slot = line % SLOTS
        step = (z_lo + 2 - (slot // 4) % 4 + 4) % 4
        sign = 1 - 2 * ((slot % 4 + slot // 16) % 2)
        dz = jnp.where(step == 2, 2 * sign, jnp.where(step == 3, -1, step))
        source = (4 * there_hi + z_lo - dz + 32) % 16
        target = 8 * slot + 2 * (source // 4) + there_core
        lane = lax.broadcasted_iota(jnp.int32, (128, QBLOCK), 1)
        for half in range(2):
            wanted = jnp.where(line // SLOTS == half, target, -1)
            for n in range(4):
                hit = jnp.where(wanted == lane + n * QBLOCK, 1.0, 0.0).astype(BF16)
                first = half * 512 + n * QBLOCK
                perm[rows(j * 128, 128), first : first + QBLOCK] = hit
        return carry

    lax.fori_loop(0, 8, order, 0)

    for far in fars:
        far.wait_recv()
    lead.wait_recv()
    total = jnp.zeros((BLOCKS, QBLOCK), F32)
    for j in range(4):
        total += far_recv[j * BLOCKS : (j + 1) * BLOCKS, :].astype(F32)
    grad = total * 0.125
    gain = OUTER_RATE * (1.0 + OUTER_MOMENTUM)
    new_row = (lead_recv[...] - gain * grad).astype(BF16)
    own_class = rem(z + 2, 4)

    def place(half, slot):
        return rows((half * SLOTS + slot) * HALF, HALF)

    own_slot = 16 * y + 4 * own_class + x
    pieces[place(0, own_slot), :] = new_row[:HALF]
    pieces[place(1, own_slot), :] = new_row[HALF:]

    def send_piece(half, slot, to):
        spot = pieces.at[place(half, slot)]
        remote(spot, spot, piece_ssem, piece_rsem.at[half * SLOTS + slot], to).start()

    def turn_piece(half, slot):
        turned[pl.ds(half * HALF * SLOTS + slot, HALF, stride=SLOTS), :] = pieces[
            place(half, slot), :
        ].astype(F32)

    def wait_piece(half, slot):
        spot = pieces.at[place(half, slot)]
        remote(spot, spot, piece_ssem, piece_rsem.at[half * SLOTS + slot], at(2)).wait_recv()

    steps = [(a, b) for a in range(4) for b in range(4)]
    length = [0, 1, 2, 1]
    steps.sort(key=lambda s: length[s[0]] + length[s[1]])
    for a, b in reversed(steps):
        dz = (0, 1, 2 * mine, -1)[b]
        if a or b:
            send_piece(0, own_slot, at(dz, 0, a))
            send_piece(1, own_slot, at(dz, a, 0))
    og_own[...] = grad.astype(BF16)

    for a, b in steps:
        for half in range(2):
            px, py = (rem(x + a, 4), y) if half == 0 else (x, rem(y + a, 4))
            there = parity(px, py)
            dz = (0, -1, -2 * there, 1)[b]
            kind = rem(z + dz + 16 + 2, 4)
            slot = 16 * py + 4 * kind + px
            if a or b:
                wait_piece(half, slot)
            for d in (2, 1, 3):
                send_piece(half, slot, at(0, d, 0) if half == 0 else at(0, 0, d))
            turn_piece(half, slot)

    ogs = []
    for j, dz in enumerate((6, -6, 2, -2)):
        ogs.append(
            remote(og_own, og_recv.at[rows(z_hi * BLOCKS, BLOCKS)], og_ssem.at[j], og_rsem.at[z_hi], at(dz))
        )
        ogs[-1].start()

    loads[3].wait()
    def second(i, carry):
        kind, p = div(i, 4), rem(i, 4)
        for d in (1, 3, 2):
            for half in range(2):
                if half == 0:
                    slot = 16 * rem(y + d, 4) + 4 * kind + p
                else:
                    slot = 16 * p + 4 * kind + rem(x + d, 4)
                wait_piece(half, slot)
                turn_piece(half, slot)
        return carry

    lax.fori_loop(0, 16, second, 0)

    for b in range(BLOCKS):
        weight[:, b * QBLOCK : (b + 1) * QBLOCK] = turned[b * SLOTS : (b + 1) * SLOTS, :].astype(BF16)
    keys = lax.dot_general(
        x_v[...], weight[...], (((1,), (1,)), ((), ())), preferred_element_type=F32
    ).astype(BF16)
    part[:, 0:QBLOCK] = jnp.concatenate([keys[:PACKED], keys[PACKED:]], axis=1)

    def spot(j):
        return part.at[:, pl.ds(j * QBLOCK, QBLOCK)]

    sends = []

    def send_keys(j, to_j, to):
        copy = remote(spot(j), spot(to_j), key_ssem.at[len(sends)], key_rsem.at[to_j], to)
        copy.start()
        sends.append(copy)

    def wait_keys(j):
        remote(spot(0), spot(j), key_ssem.at[0], key_rsem.at[j], at(2)).wait_recv()

    send_keys(0, 6, at(8))
    send_keys(0, 2, at(4))
    send_keys(0, 1, at(-4))
    send_keys(0, 3, at(other=True))

    for k in range(4):
        home = og_recv.at[pl.ds(k * BLOCKS, BLOCKS)]
        remote(home, home, og_ssem.at[0], og_rsem.at[k], at(2)).wait_recv()
    relay = remote(og_recv, og_other, ogc_sem.at[0], ogc_sem.at[1], at(other=True))
    relay.start()
    relay.wait_recv()
    for k in range(4):
        span = slice(k * BLOCKS, (k + 1) * BLOCKS)
        spread[pl.ds(2 * k + core, BLOCKS, stride=ROWS), :] = og_recv[span, :].astype(F32)
        spread[pl.ds(2 * k + 1 - core, BLOCKS, stride=ROWS), :] = og_other[span, :].astype(F32)

    def outer(step, carry):
        for k in range(4):
            b = step * 4 + k
            columns = rows(b * QBLOCK, QBLOCK)
            og = spread[rows(b * ROWS, ROWS), :]
            new_momentum = OUTER_MOMENTUM * mom_v[:, columns] + og
            base_v[:, columns] = base_v[:, columns] - OUTER_RATE * (og + OUTER_MOMENTUM * new_momentum)
            mom_v[:, columns] = new_momentum
        return carry

    lax.fori_loop(0, BLOCKS // 4, outer, 0)
    stores = [
        pltpu.make_async_copy(base_v, nb_out, out_sem.at[0]),
        pltpu.make_async_copy(mom_v, nm_out, out_sem.at[1]),
    ]
    for store in stores:
        store.start()

    for j in (1, 2):
        wait_keys(j)
        send_keys(j, j + 3, at(other=True))
    for j in (3, 4, 5):
        wait_keys(j)

    def ordered(first, last):
        held = part[:, first * QBLOCK : last * QBLOCK]
        table = perm[first * QBLOCK : last * QBLOCK, :]
        return jnp.dot(held, table, preferred_element_type=F32)

    early = ordered(0, 6)
    wait_keys(6)
    send_keys(6, 7, at(other=True))
    wait_keys(7)
    done = (early + ordered(6, 8)).astype(BF16)
    keys_v[:PACKED, :] = done[:, :512]
    keys_v[PACKED:, :] = done[:, 512:]
    stores.append(pltpu.make_async_copy(keys_v, keys_out, out_sem.at[2]))
    stores[-1].start()

    swap.wait_send()
    lead.wait_send()
    relay.wait_send()
    for copy in fars + ogs + sends:
        copy.wait_send()
    sent = pieces.at[pl.ds(0, (30 + 96) * HALF)]
    remote(sent, sent, piece_ssem, piece_rsem.at[0], at(2)).wait_send()
    for store in stores:
        store.wait()


def shards(inputs, local_weights, global_base, momentum):
    width = global_base.shape[1]
    shape = jax.ShapeDtypeStruct
    dma = pltpu.SemaphoreType.DMA
    return pl.pallas_call(
        kernel,
        name="outer_step_and_keys",
        out_shape=(
            shape((ROWS, width), F32),
            shape((ROWS, width), F32),
            shape((TOKENS, 512), BF16),
        ),
        in_specs=[pl.BlockSpec(memory_space=pl.ANY)] * 4,
        out_specs=[pl.BlockSpec(memory_space=pl.ANY)] * 3,
        scratch_shapes=[
            pltpu.VMEM((ROWS, width), F32),
            pltpu.VMEM((ROWS, width), F32),
            pltpu.VMEM((ROWS, width), F32),
            pltpu.VMEM((TOKENS, width), BF16),
            pltpu.VMEM((BLOCKS * ROWS, QBLOCK), F32),
            pltpu.VMEM((4 * BLOCKS, QBLOCK), BF16),
            pltpu.VMEM((4 * BLOCKS, QBLOCK), BF16),
            pltpu.VMEM((4 * BLOCKS, QBLOCK), BF16),
            pltpu.VMEM((4 * BLOCKS, QBLOCK), BF16),
            pltpu.VMEM((BLOCKS, QBLOCK), F32),
            pltpu.VMEM((BLOCKS, QBLOCK), F32),
            pltpu.VMEM((SLOTS * BLOCKS, QBLOCK), BF16),
            pltpu.VMEM((SLOTS * BLOCKS, QBLOCK), F32),
            pltpu.VMEM((SLOTS, width), BF16),
            pltpu.VMEM((BLOCKS, QBLOCK), BF16),
            pltpu.VMEM((4 * BLOCKS, QBLOCK), BF16),
            pltpu.VMEM((4 * BLOCKS, QBLOCK), BF16),
            pltpu.VMEM((PACKED, 8 * QBLOCK), BF16),
            pltpu.VMEM((8 * QBLOCK, 1024), BF16),
            pltpu.VMEM((TOKENS, 512), BF16),
            dma((4,)),
            dma((2,)),
            dma((4,)),
            dma((4,)),
            dma((2,)),
            dma,
            dma((2 * SLOTS,)),
            dma((4,)),
            dma((4,)),
            dma((2,)),
            dma((7,)),
            dma((8,)),
            dma((3,)),
        ],
        compiler_params=pltpu.CompilerParams(
            collective_id=0, has_side_effects=True, vmem_limit_bytes=62 * 2**20
        ),
        cost_estimate=pl.CostEstimate(flops=2 * 192 * 64 * 8192, bytes_accessed=5 * 2**20, transcendentals=1024),
    )(inputs, local_weights.reshape(ROWS, width), global_base, momentum)


def solution(mesh):
    return jax.shard_map(
        shards,
        mesh=mesh,
        in_specs=(P("fsdp", None), P("replica", "fsdp", None), P("fsdp", None), P("fsdp", None)),
        out_specs=(P("fsdp", None), P("fsdp", None), P("fsdp", None)),
        check_vma=False,
    )
```

```python
import jax
import jax.numpy as jnp
from jax import lax
from jax.experimental import pallas as pl
from jax.experimental.pallas import tpu as pltpu
from jax.sharding import PartitionSpec as P

MESH = pl.DeviceIdType.MESH
F32, BF16 = jnp.float32, jnp.bfloat16
EPSILON = 1e-06
CODE_RANGE = 127.0
OUTER_RATE = 0.7
OUTER_MOMENTUM = 0.9
QBLOCK = 128
BLOCKS = 64
ROWS = 8
HALF = 32
SLOTS = 64
TOKENS = 192
PACKED = TOKENS // 2


def rem(a, b):
    return lax.rem(a, jnp.int32(b))


def div(a, b):
    return lax.div(a, jnp.int32(b))


def device(z, core, y, x):
    return (2 * div(z, 4) + core, 16 * y + 4 * rem(z, 4) + x)


def parity(x, y):
    return 1 - 2 * rem(x + y, 2)


def rows(start, count):
    return pl.ds(pl.multiple_of(start, count), count)


def kernel(
    inp, lw, base, mom, nb_out, nm_out, keys_out,
    lw_v, base_v, mom_v, x_v, spread, core_send, core_recv, far_send, far_recv, lead_send, lead_recv,
    pieces, turned, weight, og_own, og_recv, og_other, part, perm,
    load_sem, core_sem, far_ssem, far_rsem, lead_sem, piece_ssem, piece_rsem, og_ssem, og_rsem, ogc_sem,
    key_ssem, key_rsem,
):
    replica = lax.axis_index("replica")
    fsdp = lax.axis_index("fsdp")
    z_hi, core = div(replica, 2), rem(replica, 2)
    y, z_lo, x = div(fsdp, 16), rem(div(fsdp, 4), 4), rem(fsdp, 4)
    z = 4 * z_hi + z_lo
    mine = parity(x, y)

    def at(dz=0, dy=0, dx=0, other=False):
        return device(
            rem(z + dz + 16, 16), 1 - core if other else core, rem(y + dy, 4), rem(x + dx, 4)
        )

    def remote(src, dst, ssem, rsem, to):
        return pltpu.make_async_remote_copy(
            src_ref=src, dst_ref=dst, send_sem=ssem, recv_sem=rsem, device_id=to, device_id_type=MESH
        )

    loads = [
        pltpu.make_async_copy(lw, lw_v, load_sem.at[0]),
        pltpu.make_async_copy(base, base_v, load_sem.at[1]),
        pltpu.make_async_copy(mom, mom_v, load_sem.at[2]),
        pltpu.make_async_copy(inp, x_v, load_sem.at[3]),
    ]
    for load in loads:
        load.start()

    barrier = pltpu.get_barrier_semaphore()
    greeted = 0

    def greet(to):
        pl.semaphore_signal(barrier, inc=1, device_id=to, device_id_type=MESH)

    for dz in (6, -6, 2, -2):
        greet(at(dz))
        greeted += 1
    for dx in range(4):
        there = parity(rem(x + dx, 4), y)
        for dz in (0, 1, -1, None):
            if dx or dz != 0:
                greet(at(-2 * there if dz is None else -dz, 0, dx))
                greeted += 1
    for dy in range(1, 4):
        there = parity(x, rem(y + dy, 4))
        for dz in (0, 1, -1, None):
            greet(at(-2 * there if dz is None else -dz, dy))
            greeted += 1
    greet(at(other=True))
    greeted += 1

    loads[0].wait()
    loads[1].wait()

    def quantize(step, carry):
        for k in range(4):
            b = step * 4 + k
            columns = rows(b * QBLOCK, QBLOCK)
            pseudo = base_v[:, columns] - lw_v[:, columns]
            peak = jnp.max(jnp.abs(pseudo), axis=-1, keepdims=True)
            scale = jnp.exp2(jnp.ceil(jnp.log2((peak + EPSILON) / CODE_RANGE)))
            scale = scale.astype(BF16).astype(F32)
            codes = jnp.floor(pseudo / scale + 0.5).astype(BF16).astype(F32)
            spread[rows(b * ROWS, ROWS), :] = codes * scale
        return carry

    lax.fori_loop(0, BLOCKS // 4, quantize, 0)

    def row(ref, q):
        return ref[pl.ds(q, BLOCKS, stride=ROWS), :]

    for k in range(4):
        core_send[k * BLOCKS : (k + 1) * BLOCKS, :] = row(spread, 2 * k + 1 - core).astype(BF16)

    pl.semaphore_wait(barrier, greeted)

    swap = remote(core_send, core_recv, core_sem.at[0], core_sem.at[1], at(other=True))
    swap.start()

    loads[2].wait()
    lead_q = 2 * div(rem(z + 2, 16), 4) + core
    keep = [row(spread, 2 * k + core) for k in range(4)]

    def lead_rows(step, carry):
        for k in range(4):
            b = step * 4 + k
            columns = rows(b * QBLOCK, QBLOCK)
            turned[rows(b * ROWS, ROWS), :] = base_v[:, columns] - (
                OUTER_RATE * OUTER_MOMENTUM * OUTER_MOMENTUM
            ) * mom_v[:, columns]
        return carry

    lax.fori_loop(0, BLOCKS // 4, lead_rows, 0)
    lead_send[...] = row(turned, lead_q)

    swap.wait_recv()
    for k in range(4):
        part_sum = keep[k] + core_recv[k * BLOCKS : (k + 1) * BLOCKS, :].astype(F32)
        far_send[k * BLOCKS : (k + 1) * BLOCKS, :] = part_sum.astype(BF16)
    fars = []
    for j, dz in enumerate((6, -6, 2, -2)):
        k = div(rem(z + dz + 16, 16), 4)
        fars.append(
            remote(
                far_send.at[rows(k * BLOCKS, BLOCKS)],
                far_recv.at[pl.ds(j * BLOCKS, BLOCKS)],
                far_ssem.at[j],
                far_rsem.at[j],
                at(dz),
            )
        )
        fars[-1].start()
    lead = remote(lead_send, lead_recv, lead_sem.at[0], lead_sem.at[1], at(2))
    lead.start()

    def order(j, carry):
        late = jnp.where(j >= 6, 1, 0)
        other = late * (j - 6) + (1 - late) * div(j, 3)
        turn = late * 2 + (1 - late) * rem(j * j, 3) * (1 + 2 * jnp.where(rem(j, 3) == 2, 1, 0))
        there_hi = z_hi + turn
        there_core = rem(core + other, 2)
        line = lax.broadcasted_iota(jnp.int32, (128, QBLOCK), 0)
        slot = line % SLOTS
        step = (z_lo + 2 - (slot // 4) % 4 + 4) % 4
        sign = 1 - 2 * ((slot % 4 + slot // 16) % 2)
        dz = jnp.where(step == 2, 2 * sign, jnp.where(step == 3, -1, step))
        source = (4 * there_hi + z_lo - dz + 32) % 16
        target = 8 * slot + 2 * (source // 4) + there_core
        lane = lax.broadcasted_iota(jnp.int32, (128, QBLOCK), 1)
        for half in range(2):
            wanted = jnp.where(line // SLOTS == half, target, -1)
            for n in range(4):
                hit = jnp.where(wanted == lane + n * QBLOCK, 1.0, 0.0).astype(BF16)
                first = half * 512 + n * QBLOCK
                perm[rows(j * 128, 128), first : first + QBLOCK] = hit
        return carry

    lax.fori_loop(0, 8, order, 0)

    for far in fars:
        far.wait_recv()
    lead.wait_recv()
    total = jnp.zeros((BLOCKS, QBLOCK), F32)
    for j in range(4):
        total += far_recv[j * BLOCKS : (j + 1) * BLOCKS, :].astype(F32)
    grad = total * 0.125
    gain = OUTER_RATE * (1.0 + OUTER_MOMENTUM)
    new_row = (lead_recv[...] - gain * grad).astype(BF16)
    own_class = rem(z + 2, 4)

    def place(half, slot):
        return rows((half * SLOTS + slot) * HALF, HALF)

    own_slot = 16 * y + 4 * own_class + x
    pieces[place(0, own_slot), :] = new_row[:HALF]
    pieces[place(1, own_slot), :] = new_row[HALF:]

    def send_piece(half, slot, to):
        spot = pieces.at[place(half, slot)]
        remote(spot, spot, piece_ssem, piece_rsem.at[half * SLOTS + slot], to).start()

    def turn_piece(half, slot):
        turned[pl.ds(half * HALF * SLOTS + slot, HALF, stride=SLOTS), :] = pieces[
            place(half, slot), :
        ].astype(F32)

    def wait_piece(half, slot):
        spot = pieces.at[place(half, slot)]
        remote(spot, spot, piece_ssem, piece_rsem.at[half * SLOTS + slot], at(2)).wait_recv()

    steps = [(a, b) for a in range(4) for b in range(4)]
    length = [0, 1, 2, 1]
    steps.sort(key=lambda s: length[s[0]] + length[s[1]])
    for a, b in steps:
        dz = (0, 1, 2 * mine, -1)[b]
        if a or b:
            send_piece(0, own_slot, at(dz, 0, a))
            send_piece(1, own_slot, at(dz, a, 0))
    og_own[...] = grad.astype(BF16)

    for a, b in steps:
        for half in range(2):
            px, py = (rem(x + a, 4), y) if half == 0 else (x, rem(y + a, 4))
            there = parity(px, py)
            dz = (0, -1, -2 * there, 1)[b]
            kind = rem(z + dz + 16 + 2, 4)
            slot = 16 * py + 4 * kind + px
            if a or b:
                wait_piece(half, slot)
            for d in (2, 1, 3):
                send_piece(half, slot, at(0, d, 0) if half == 0 else at(0, 0, d))
            turn_piece(half, slot)

    ogs = []
    for j, dz in enumerate((6, -6, 2, -2)):
        ogs.append(
            remote(og_own, og_recv.at[rows(z_hi * BLOCKS, BLOCKS)], og_ssem.at[j], og_rsem.at[z_hi], at(dz))
        )
        ogs[-1].start()

    loads[3].wait()
    def second(i, carry):
        kind, p = div(i, 4), rem(i, 4)
        for d in (1, 3, 2):
            for half in range(2):
                if half == 0:
                    slot = 16 * rem(y + d, 4) + 4 * kind + p
                else:
                    slot = 16 * p + 4 * kind + rem(x + d, 4)
                wait_piece(half, slot)
                turn_piece(half, slot)
        return carry

    lax.fori_loop(0, 16, second, 0)

    for b in range(BLOCKS):
        weight[:, b * QBLOCK : (b + 1) * QBLOCK] = turned[b * SLOTS : (b + 1) * SLOTS, :].astype(BF16)
    keys = lax.dot_general(
        x_v[...], weight[...], (((1,), (1,)), ((), ())), preferred_element_type=F32
    ).astype(BF16)
    part[:, 0:QBLOCK] = jnp.concatenate([keys[:PACKED], keys[PACKED:]], axis=1)

    def spot(j):
        return part.at[:, pl.ds(j * QBLOCK, QBLOCK)]

    sends = []

    def send_keys(j, to_j, to):
        copy = remote(spot(j), spot(to_j), key_ssem.at[len(sends)], key_rsem.at[to_j], to)
        copy.start()
        sends.append(copy)

    def wait_keys(j):
        remote(spot(0), spot(j), key_ssem.at[0], key_rsem.at[j], at(2)).wait_recv()

    send_keys(0, 6, at(8))
    send_keys(0, 2, at(4))
    send_keys(0, 1, at(-4))
    send_keys(0, 3, at(other=True))

    for k in range(4):
        home = og_recv.at[pl.ds(k * BLOCKS, BLOCKS)]
        remote(home, home, og_ssem.at[0], og_rsem.at[k], at(2)).wait_recv()
    relay = remote(og_recv, og_other, ogc_sem.at[0], ogc_sem.at[1], at(other=True))
    relay.start()
    relay.wait_recv()
    for k in range(4):
        span = slice(k * BLOCKS, (k + 1) * BLOCKS)
        spread[pl.ds(2 * k + core, BLOCKS, stride=ROWS), :] = og_recv[span, :].astype(F32)
        spread[pl.ds(2 * k + 1 - core, BLOCKS, stride=ROWS), :] = og_other[span, :].astype(F32)

    def outer(step, carry):
        for k in range(4):
            b = step * 4 + k
            columns = rows(b * QBLOCK, QBLOCK)
            og = spread[rows(b * ROWS, ROWS), :]
            new_momentum = OUTER_MOMENTUM * mom_v[:, columns] + og
            nb_out[:, columns] = base_v[:, columns] - OUTER_RATE * (og + OUTER_MOMENTUM * new_momentum)
            nm_out[:, columns] = new_momentum
        return carry

    lax.fori_loop(0, BLOCKS // 4, outer, 0)
    for j in (1, 2):
        wait_keys(j)
        send_keys(j, j + 3, at(other=True))
    for j in (3, 4, 5):
        wait_keys(j)

    def ordered(first, last):
        held = part[:, first * QBLOCK : last * QBLOCK]
        table = perm[first * QBLOCK : last * QBLOCK, :]
        return jnp.dot(held, table, preferred_element_type=F32)

    early = ordered(0, 6)
    wait_keys(6)
    send_keys(6, 7, at(other=True))
    wait_keys(7)
    done = (early + ordered(6, 8)).astype(BF16)
    keys_out[:PACKED, :] = done[:, :512]
    keys_out[PACKED:, :] = done[:, 512:]

    swap.wait_send()
    lead.wait_send()
    relay.wait_send()
    for copy in fars + ogs + sends:
        copy.wait_send()
    sent = pieces.at[pl.ds(0, (30 + 96) * HALF)]
    remote(sent, sent, piece_ssem, piece_rsem.at[0], at(2)).wait_send()


def store(nb, nm, keys, nb_out, nm_out, keys_out, sem):
    copies = [
        pltpu.make_async_copy(here, there, sem.at[j])
        for j, (here, there) in enumerate(((keys, keys_out), (nb, nb_out), (nm, nm_out)))
    ]
    for copy in copies:
        copy.start()
    for copy in copies:
        copy.wait()


def shards(inputs, local_weights, global_base, momentum):
    width = global_base.shape[1]
    shape = jax.ShapeDtypeStruct
    dma = pltpu.SemaphoreType.DMA
    inputs, local_weights, global_base, momentum = (
        pltpu.with_memory_space_constraint(a, pltpu.HBM)
        for a in (inputs, local_weights.reshape(ROWS, width), global_base, momentum)
    )
    results = pl.pallas_call(
        kernel,
        name="outer_step_and_keys",
        out_shape=(
            pltpu.VMEM((ROWS, width), F32),
            pltpu.VMEM((ROWS, width), F32),
            pltpu.VMEM((TOKENS, 512), BF16),
        ),
        in_specs=[pl.BlockSpec(memory_space=pl.ANY)] * 4,
        out_specs=[pl.BlockSpec(memory_space=pltpu.VMEM)] * 3,
        scratch_shapes=[
            pltpu.VMEM((ROWS, width), F32),
            pltpu.VMEM((ROWS, width), F32),
            pltpu.VMEM((ROWS, width), F32),
            pltpu.VMEM((TOKENS, width), BF16),
            pltpu.VMEM((BLOCKS * ROWS, QBLOCK), F32),
            pltpu.VMEM((4 * BLOCKS, QBLOCK), BF16),
            pltpu.VMEM((4 * BLOCKS, QBLOCK), BF16),
            pltpu.VMEM((4 * BLOCKS, QBLOCK), BF16),
            pltpu.VMEM((4 * BLOCKS, QBLOCK), BF16),
            pltpu.VMEM((BLOCKS, QBLOCK), F32),
            pltpu.VMEM((BLOCKS, QBLOCK), F32),
            pltpu.VMEM((SLOTS * BLOCKS, QBLOCK), BF16),
            pltpu.VMEM((SLOTS * BLOCKS, QBLOCK), F32),
            pltpu.VMEM((SLOTS, width), BF16),
            pltpu.VMEM((BLOCKS, QBLOCK), BF16),
            pltpu.VMEM((4 * BLOCKS, QBLOCK), BF16),
            pltpu.VMEM((4 * BLOCKS, QBLOCK), BF16),
            pltpu.VMEM((PACKED, 8 * QBLOCK), BF16),
            pltpu.VMEM((8 * QBLOCK, 1024), BF16),
            dma((4,)),
            dma((2,)),
            dma((4,)),
            dma((4,)),
            dma((2,)),
            dma,
            dma((2 * SLOTS,)),
            dma((4,)),
            dma((4,)),
            dma((2,)),
            dma((7,)),
            dma((8,)),
        ],
        compiler_params=pltpu.CompilerParams(
            collective_id=0, has_side_effects=True, vmem_limit_bytes=40 * 2**20
        ),
        cost_estimate=pl.CostEstimate(flops=2 * 192 * 64 * 8192, bytes_accessed=5 * 2**20, transcendentals=1024),
    )(inputs, local_weights, global_base, momentum)
    results = [pltpu.with_memory_space_constraint(a, pltpu.VMEM) for a in results]
    return pl.pallas_call(
        store,
        name="store_results",
        out_shape=tuple(shape(a.shape, a.dtype) for a in results),
        in_specs=[pl.BlockSpec(memory_space=pltpu.VMEM)] * 3,
        out_specs=[pl.BlockSpec(memory_space=pltpu.HBM)] * 3,
        scratch_shapes=[dma((3,))],
        compiler_params=pltpu.CompilerParams(vmem_limit_bytes=2 * 2**20),
    )(*results)


def solution(mesh):
    return jax.shard_map(
        shards,
        mesh=mesh,
        in_specs=(P("fsdp", None), P("replica", "fsdp", None), P("fsdp", None), P("fsdp", None)),
        out_specs=(P("fsdp", None), P("fsdp", None), P("fsdp", None)),
        check_vma=False,
    )
```

```python
import jax
import jax.numpy as jnp
from jax import lax
from jax.experimental import pallas as pl
from jax.experimental.pallas import tpu as pltpu
from jax.sharding import PartitionSpec as P

MESH = pl.DeviceIdType.MESH
F32, BF16 = jnp.float32, jnp.bfloat16
EPSILON = 1e-06
CODE_RANGE = 127.0
OUTER_RATE = 0.7
OUTER_MOMENTUM = 0.9
QBLOCK = 128
BLOCKS = 64
ROWS = 8
HALF = 32
SLOTS = 64
TOKENS = 192
PACKED = TOKENS // 2


def rem(a, b):
    return lax.rem(a, jnp.int32(b))


def div(a, b):
    return lax.div(a, jnp.int32(b))


def device(z, core, y, x):
    return (2 * div(z, 4) + core, 16 * y + 4 * rem(z, 4) + x)


def parity(x, y):
    return 1 - 2 * rem(x + y, 2)


def rows(start, count):
    return pl.ds(pl.multiple_of(start, count), count)


def kernel(
    inp, lw, base, mom, nb_out, nm_out, keys_out,
    lw_v, base_v, mom_v, x_v, spread, core_send, core_recv, far_send, far_recv, lead_send, lead_recv,
    pieces, turned, weight, og_own, og_recv, og_other, part, perm,
    load_sem, core_sem, far_ssem, far_rsem, lead_sem, piece_ssem, piece_rsem, near_sem, far_sem, og_ssem, og_rsem, ogc_sem,
    key_ssem, key_rsem,
):
    replica = lax.axis_index("replica")
    fsdp = lax.axis_index("fsdp")
    z_hi, core = div(replica, 2), rem(replica, 2)
    y, z_lo, x = div(fsdp, 16), rem(div(fsdp, 4), 4), rem(fsdp, 4)
    z = 4 * z_hi + z_lo
    mine = parity(x, y)

    def at(dz=0, dy=0, dx=0, other=False):
        return device(
            rem(z + dz + 16, 16), 1 - core if other else core, rem(y + dy, 4), rem(x + dx, 4)
        )

    def remote(src, dst, ssem, rsem, to):
        return pltpu.make_async_remote_copy(
            src_ref=src, dst_ref=dst, send_sem=ssem, recv_sem=rsem, device_id=to, device_id_type=MESH
        )

    loads = [
        pltpu.make_async_copy(lw, lw_v, load_sem.at[0]),
        pltpu.make_async_copy(base, base_v, load_sem.at[1]),
        pltpu.make_async_copy(mom, mom_v, load_sem.at[2]),
        pltpu.make_async_copy(inp, x_v, load_sem.at[3]),
    ]
    barrier = pltpu.get_barrier_semaphore()
    greeted = 0

    def greet(to):
        pl.semaphore_signal(barrier, inc=1, device_id=to, device_id_type=MESH)

    for dz in (6, -6):
        greet(at(dz))
        greeted += 1
    for load in loads[:2]:
        load.start()
    for dz in (2, -2):
        greet(at(dz))
        greeted += 1
    for dx in range(4):
        there = parity(rem(x + dx, 4), y)
        for dz in (0, 1, -1, None):
            if dx or dz != 0:
                greet(at(-2 * there if dz is None else -dz, 0, dx))
                greeted += 1
    for dy in range(1, 4):
        there = parity(x, rem(y + dy, 4))
        for dz in (0, 1, -1, None):
            greet(at(-2 * there if dz is None else -dz, dy))
            greeted += 1
        for dx in range(1, 4):
            greet(at(0, dy, dx))
            greeted += 1
    greet(at(other=True))
    greeted += 1

    loads[0].wait()
    loads[1].wait()
    loads[2].start()
    loads[3].start()

    def quantize(step, carry):
        for k in range(16):
            b = step * 16 + k
            columns = rows(b * QBLOCK, QBLOCK)
            pseudo = base_v[:, columns] - lw_v[:, columns]
            peak = jnp.max(jnp.abs(pseudo), axis=-1, keepdims=True)
            scale = jnp.exp2(jnp.ceil(jnp.log2((peak + EPSILON) / CODE_RANGE)))
            scale = scale.astype(BF16).astype(F32)
            codes = jnp.floor(pseudo / scale + 0.5).astype(BF16).astype(F32)
            spread[rows(b * ROWS, ROWS), :] = codes * scale
        return carry

    lax.fori_loop(0, BLOCKS // 16, quantize, 0)

    def row(ref, q):
        return ref[pl.ds(q, BLOCKS, stride=ROWS), :]

    for k in range(4):
        core_send[k * BLOCKS : (k + 1) * BLOCKS, :] = row(spread, 2 * k + 1 - core).astype(BF16)

    pl.semaphore_wait(barrier, greeted)

    swap = remote(core_send, core_recv, core_sem.at[0], core_sem.at[1], at(other=True))
    swap.start()

    loads[2].wait()
    lead_q = 2 * div(rem(z + 2, 16), 4) + core
    keep = [row(spread, 2 * k + core) for k in range(4)]

    def lead_rows(step, carry):
        for k in range(4):
            b = step * 4 + k
            columns = rows(b * QBLOCK, QBLOCK)
            turned[rows(b * ROWS, ROWS), :] = base_v[:, columns] - (
                OUTER_RATE * OUTER_MOMENTUM * OUTER_MOMENTUM
            ) * mom_v[:, columns]
        return carry

    lax.fori_loop(0, BLOCKS // 4, lead_rows, 0)
    lead_send[...] = row(turned, lead_q)

    swap.wait_recv()
    for k in range(4):
        part_sum = keep[k] + core_recv[k * BLOCKS : (k + 1) * BLOCKS, :].astype(F32)
        far_send[k * BLOCKS : (k + 1) * BLOCKS, :] = part_sum.astype(BF16)
    fars = []
    for j, dz in enumerate((6, -6, 2, -2)):
        k = div(rem(z + dz + 16, 16), 4)
        fars.append(
            remote(
                far_send.at[rows(k * BLOCKS, BLOCKS)],
                far_recv.at[pl.ds(j * BLOCKS, BLOCKS)],
                far_ssem.at[j],
                far_rsem.at[j],
                at(dz),
            )
        )
        fars[-1].start()
    lead = remote(lead_send, lead_recv, lead_sem.at[0], lead_sem.at[1], at(2))
    lead.start()

    def order(j, carry):
        late = jnp.where(j >= 6, 1, 0)
        other = late * (j - 6) + (1 - late) * div(j, 3)
        turn = late * 2 + (1 - late) * rem(j * j, 3) * (1 + 2 * jnp.where(rem(j, 3) == 2, 1, 0))
        there_hi = z_hi + turn
        there_core = rem(core + other, 2)
        line = lax.broadcasted_iota(jnp.int32, (128, QBLOCK), 0)
        slot = line % SLOTS
        step = (z_lo + 2 - (slot // 4) % 4 + 4) % 4
        sign = 1 - 2 * ((slot % 4 + slot // 16) % 2)
        dz = jnp.where(step == 2, 2 * sign, jnp.where(step == 3, -1, step))
        source = (4 * there_hi + z_lo - dz + 32) % 16
        target = 8 * slot + 2 * (source // 4) + there_core
        lane = lax.broadcasted_iota(jnp.int32, (128, QBLOCK), 1)
        for half in range(2):
            wanted = jnp.where(line // SLOTS == half, target, -1)
            for n in range(4):
                hit = jnp.where(wanted == lane + n * QBLOCK, 1.0, 0.0).astype(BF16)
                first = half * 512 + n * QBLOCK
                perm[rows(j * 128, 128), first : first + QBLOCK] = hit
        return carry

    lax.fori_loop(0, 8, order, 0)

    for far in fars:
        far.wait_recv()
    lead.wait_recv()
    total = jnp.zeros((BLOCKS, QBLOCK), F32)
    for j in range(4):
        total += far_recv[j * BLOCKS : (j + 1) * BLOCKS, :].astype(F32)
    grad = total * 0.125
    gain = OUTER_RATE * (1.0 + OUTER_MOMENTUM)
    new_row = (lead_recv[...] - gain * grad).astype(BF16)
    own_class = rem(z + 2, 4)

    def place(half, slot):
        return rows((half * SLOTS + slot) * HALF, HALF)

    own_slot = 16 * y + 4 * own_class + x
    pieces[place(0, own_slot), :] = new_row[:HALF]
    pieces[place(1, own_slot), :] = new_row[HALF:]

    def first_path(kind, py, px):
        return rem(rem(px + py + kind, 4), 3)

    def choose(path, options):
        return tuple(
            jnp.where(path == 0, a, jnp.where(path == 1, b, c)) for a, b, c in zip(*options)
        )

    def send_piece(half, slot, to, sem):
        spot = pieces.at[place(half, slot)]
        remote(spot, spot, piece_ssem, sem, to).start()

    steps = [(a, b) for a in range(4) for b in range(4)]
    length = [0, 1, 2, 1]
    steps.sort(key=lambda s: length[s[0]] + length[s[1]])
    for a, b in steps[1:]:
        dz = (0, 1, 2 * mine, -1)[b]
        options = (at(dz, 0, a), at(dz, a, 0), at(0, a, b))
        for half in range(2):
            path = rem(first_path(own_class, y, x) + half, 3)
            send_piece(half, own_slot, choose(path, options), piece_rsem.at[half * SLOTS + own_slot])
    og_own[...] = grad.astype(BF16)

    third = (
        (at(0, 2), at(0, 1), at(0, 3)),
        (at(0, 0, 2), at(0, 0, 1), at(0, 0, 3)),
        (at(1), at(-1)),
    )
    at_2, at_m2 = at(2), at(-2)

    for a, b in steps:
        for path in range(3):
            px = x if path == 1 else rem(x + (a if path == 0 else b), 4)
            py = y if path == 0 else rem(y + a, 4)
            there = parity(px, py)
            dz = 0 if path == 2 else (0, -1, -2 * there, 1)[b]
            kind = rem(z + dz + 16 + 2, 4)
            slot = 16 * py + 4 * kind + px
            half = rem(path + 3 - first_path(kind, py, px), 3)

            @pl.when(half < 2)
            def _(path=path, half=half, slot=slot, there=there, own=not (a or b)):
                if not own:
                    spot = pieces.at[place(half, slot)]
                    remote(spot, spot, piece_ssem, piece_rsem.at[half * SLOTS + slot], at(2)).wait_recv()
                ends = third[path]
                if path == 2:
                    far_end = tuple(jnp.where(there == 1, p, m) for p, m in zip(at_2, at_m2))
                    ends = (far_end, *ends)
                for end, sem in zip(ends, (far_sem, near_sem, near_sem)):
                    send_piece(half, slot, end, sem)

    ogs = []
    for j, dz in enumerate((6, -6, 2, -2)):
        ogs.append(
            remote(og_own, og_recv.at[rows(z_hi * BLOCKS, BLOCKS)], og_ssem.at[j], og_rsem.at[z_hi], at(dz))
        )
        ogs[-1].start()

    loads[3].wait()
    def wait_pieces(count, sem):
        spots = pieces.at[pl.ds(0, count * HALF)]
        remote(spots, spots, piece_ssem, sem, at(2)).wait_recv()

    wait_pieces(64, near_sem)
    wait_pieces(32, far_sem)

    for half in range(2):
        for slot in range(0, SLOTS, 16):
            group = pieces[pl.ds((half * SLOTS + slot) * HALF, 16 * HALF), :]
            group = jnp.transpose(group.reshape(16, HALF, QBLOCK), (1, 0, 2))
            for b in range(HALF):
                first = (half * HALF + b) * QBLOCK
                weight[slot : slot + 16, first : first + QBLOCK] = group[b]
    keys = lax.dot_general(
        x_v[...], weight[...], (((1,), (1,)), ((), ())), preferred_element_type=F32
    ).astype(BF16)
    part[:, 0:QBLOCK] = jnp.concatenate([keys[:PACKED], keys[PACKED:]], axis=1)

    def spot(j):
        return part.at[:, pl.ds(j * QBLOCK, QBLOCK)]

    sends = []

    def send_keys(j, to_j, to):
        copy = remote(spot(j), spot(to_j), key_ssem.at[len(sends)], key_rsem.at[to_j], to)
        copy.start()
        sends.append(copy)

    def wait_keys(j):
        remote(spot(0), spot(j), key_ssem.at[0], key_rsem.at[j], at(2)).wait_recv()

    send_keys(0, 6, at(8))
    send_keys(0, 2, at(4))
    send_keys(0, 1, at(-4))
    send_keys(0, 3, at(other=True))

    for k in range(4):
        home = og_recv.at[pl.ds(k * BLOCKS, BLOCKS)]
        remote(home, home, og_ssem.at[0], og_rsem.at[k], at(2)).wait_recv()
    relay = remote(og_recv, og_other, ogc_sem.at[0], ogc_sem.at[1], at(other=True))
    relay.start()
    relay.wait_recv()
    for k in range(4):
        span = slice(k * BLOCKS, (k + 1) * BLOCKS)
        spread[pl.ds(2 * k + core, BLOCKS, stride=ROWS), :] = og_recv[span, :].astype(F32)
        spread[pl.ds(2 * k + 1 - core, BLOCKS, stride=ROWS), :] = og_other[span, :].astype(F32)

    def outer(step, carry):
        for k in range(4):
            b = step * 4 + k
            columns = rows(b * QBLOCK, QBLOCK)
            og = spread[rows(b * ROWS, ROWS), :]
            new_momentum = OUTER_MOMENTUM * mom_v[:, columns] + og
            nb_out[:, columns] = base_v[:, columns] - OUTER_RATE * (og + OUTER_MOMENTUM * new_momentum)
            nm_out[:, columns] = new_momentum
        return carry

    lax.fori_loop(0, BLOCKS // 4, outer, 0)
    for j in (1, 2):
        wait_keys(j)
        send_keys(j, j + 3, at(other=True))
    for j in (3, 4, 5):
        wait_keys(j)

    def ordered(first, last):
        held = part[:, first * QBLOCK : last * QBLOCK]
        table = perm[first * QBLOCK : last * QBLOCK, :]
        return jnp.dot(held, table, preferred_element_type=F32)

    early = ordered(0, 6)
    wait_keys(6)
    send_keys(6, 7, at(other=True))
    wait_keys(7)
    done = (early + ordered(6, 8)).astype(BF16)
    keys_out[:PACKED, :] = done[:, :512]
    keys_out[PACKED:, :] = done[:, 512:]

    swap.wait_send()
    lead.wait_send()
    relay.wait_send()
    for copy in fars + ogs + sends:
        copy.wait_send()
    sent = pieces.at[pl.ds(0, (30 + 96) * HALF)]
    remote(sent, sent, piece_ssem, piece_rsem.at[0], at(2)).wait_send()


def store(nb, nm, keys, nb_out, nm_out, keys_out, sem):
    copies = [
        pltpu.make_async_copy(here, there, sem.at[j])
        for j, (here, there) in enumerate(((keys, keys_out), (nb, nb_out), (nm, nm_out)))
    ]
    for copy in copies:
        copy.start()
    for copy in copies:
        copy.wait()


def shards(inputs, local_weights, global_base, momentum):
    width = global_base.shape[1]
    shape = jax.ShapeDtypeStruct
    dma = pltpu.SemaphoreType.DMA
    inputs, local_weights, global_base, momentum = (
        pltpu.with_memory_space_constraint(a, pltpu.HBM)
        for a in (inputs, local_weights.reshape(ROWS, width), global_base, momentum)
    )
    results = pl.pallas_call(
        kernel,
        name="outer_step_and_keys",
        out_shape=(
            pltpu.VMEM((ROWS, width), F32),
            pltpu.VMEM((ROWS, width), F32),
            pltpu.VMEM((TOKENS, 512), BF16),
        ),
        in_specs=[pl.BlockSpec(memory_space=pl.ANY)] * 4,
        out_specs=[pl.BlockSpec(memory_space=pltpu.VMEM)] * 3,
        scratch_shapes=[
            pltpu.VMEM((ROWS, width), F32),
            pltpu.VMEM((ROWS, width), F32),
            pltpu.VMEM((ROWS, width), F32),
            pltpu.VMEM((TOKENS, width), BF16),
            pltpu.VMEM((BLOCKS * ROWS, QBLOCK), F32),
            pltpu.VMEM((4 * BLOCKS, QBLOCK), BF16),
            pltpu.VMEM((4 * BLOCKS, QBLOCK), BF16),
            pltpu.VMEM((4 * BLOCKS, QBLOCK), BF16),
            pltpu.VMEM((4 * BLOCKS, QBLOCK), BF16),
            pltpu.VMEM((BLOCKS, QBLOCK), F32),
            pltpu.VMEM((BLOCKS, QBLOCK), F32),
            pltpu.VMEM((SLOTS * BLOCKS, QBLOCK), BF16),
            pltpu.VMEM((BLOCKS * ROWS, QBLOCK), F32),
            pltpu.VMEM((SLOTS, width), BF16),
            pltpu.VMEM((BLOCKS, QBLOCK), BF16),
            pltpu.VMEM((4 * BLOCKS, QBLOCK), BF16),
            pltpu.VMEM((4 * BLOCKS, QBLOCK), BF16),
            pltpu.VMEM((PACKED, 8 * QBLOCK), BF16),
            pltpu.VMEM((8 * QBLOCK, 1024), BF16),
            dma((4,)),
            dma((2,)),
            dma((4,)),
            dma((4,)),
            dma((2,)),
            dma,
            dma((2 * SLOTS,)),
            dma,
            dma,
            dma((4,)),
            dma((4,)),
            dma((2,)),
            dma((7,)),
            dma((8,)),
        ],
        compiler_params=pltpu.CompilerParams(
            collective_id=0, has_side_effects=True, vmem_limit_bytes=40 * 2**20
        ),
        cost_estimate=pl.CostEstimate(flops=2 * 192 * 64 * 8192, bytes_accessed=5 * 2**20, transcendentals=1024),
    )(inputs, local_weights, global_base, momentum)
    results = [pltpu.with_memory_space_constraint(a, pltpu.VMEM) for a in results]
    return pl.pallas_call(
        store,
        name="store_results",
        out_shape=tuple(shape(a.shape, a.dtype) for a in results),
        in_specs=[pl.BlockSpec(memory_space=pltpu.VMEM)] * 3,
        out_specs=[pl.BlockSpec(memory_space=pltpu.HBM)] * 3,
        scratch_shapes=[dma((3,))],
        compiler_params=pltpu.CompilerParams(vmem_limit_bytes=2 * 2**20),
    )(*results)


def solution(mesh):
    return jax.shard_map(
        shards,
        mesh=mesh,
        in_specs=(P("fsdp", None), P("replica", "fsdp", None), P("fsdp", None), P("fsdp", None)),
        out_specs=(P("fsdp", None), P("fsdp", None), P("fsdp", None)),
        check_vma=False,
    )
```

```python
import jax
import jax.numpy as jnp
from jax import lax
from jax.experimental import pallas as pl
from jax.experimental.pallas import tpu as pltpu
from jax.sharding import PartitionSpec as P

MESH = pl.DeviceIdType.MESH
F32, BF16 = jnp.float32, jnp.bfloat16
EPSILON = 1e-06
CODE_RANGE = 127.0
OUTER_RATE = 0.7
OUTER_MOMENTUM = 0.9
QBLOCK = 128
BLOCKS = 64
ROWS = 8
HALF = 32
SLOTS = 64
TOKENS = 192
PACKED = TOKENS // 2


def rem(a, b):
    return lax.rem(a, jnp.int32(b))


def div(a, b):
    return lax.div(a, jnp.int32(b))


def device(z, core, y, x):
    return (2 * div(z, 4) + core, 16 * y + 4 * rem(z, 4) + x)


def parity(x, y):
    return 1 - 2 * rem(x + y, 2)


def rows(start, count):
    return pl.ds(pl.multiple_of(start, count), count)


def kernel(
    inp, lw, base, mom, nb_out, nm_out, keys_out,
    lw_v, base_v, mom_v, x_v, spread, core_send, core_recv, far_send, far_recv, lead_send, lead_recv,
    pieces, turned, weight, og_own, og_recv, og_other, part, perm,
    load_sem, core_sem, far_ssem, far_rsem, lead_sem, piece_ssem, piece_rsem, near_sem, far_sem, og_ssem, og_rsem, ogc_sem,
    key_ssem, key_rsem,
):
    replica = lax.axis_index("replica")
    fsdp = lax.axis_index("fsdp")
    z_hi, core = div(replica, 2), rem(replica, 2)
    y, z_lo, x = div(fsdp, 16), rem(div(fsdp, 4), 4), rem(fsdp, 4)
    z = 4 * z_hi + z_lo
    mine = parity(x, y)

    def at(dz=0, dy=0, dx=0, other=False):
        return device(
            rem(z + dz + 16, 16), 1 - core if other else core, rem(y + dy, 4), rem(x + dx, 4)
        )

    def remote(src, dst, ssem, rsem, to):
        return pltpu.make_async_remote_copy(
            src_ref=src, dst_ref=dst, send_sem=ssem, recv_sem=rsem, device_id=to, device_id_type=MESH
        )

    loads = [
        pltpu.make_async_copy(lw, lw_v, load_sem.at[0]),
        pltpu.make_async_copy(base, base_v, load_sem.at[1]),
        pltpu.make_async_copy(mom, mom_v, load_sem.at[2]),
        pltpu.make_async_copy(inp, x_v, load_sem.at[3]),
    ]
    barrier = pltpu.get_barrier_semaphore()
    greeted = 0

    def greet(to):
        pl.semaphore_signal(barrier, inc=1, device_id=to, device_id_type=MESH)

    for dz in (6, -6):
        greet(at(dz))
        greeted += 1
    for load in loads[:2]:
        load.start()
    for dz in (2, -2):
        greet(at(dz))
        greeted += 1
    for dx in range(4):
        there = parity(rem(x + dx, 4), y)
        for dz in (0, 1, -1, None):
            if dx or dz != 0:
                greet(at(-2 * there if dz is None else -dz, 0, dx))
                greeted += 1
    for dy in range(1, 4):
        there = parity(x, rem(y + dy, 4))
        for dz in (0, 1, -1, None):
            greet(at(-2 * there if dz is None else -dz, dy))
            greeted += 1
        for dx in range(1, 4):
            greet(at(0, dy, dx))
            greeted += 1
    greet(at(other=True))
    greeted += 1

    loads[0].wait()
    loads[1].wait()
    loads[2].start()
    loads[3].start()

    def quantize(step, carry):
        for k in range(16):
            b = step * 16 + k
            columns = rows(b * QBLOCK, QBLOCK)
            pseudo = base_v[:, columns] - lw_v[:, columns]
            peak = jnp.max(jnp.abs(pseudo), axis=-1, keepdims=True)
            scale = jnp.exp2(jnp.ceil(jnp.log2((peak + EPSILON) / CODE_RANGE)))
            scale = scale.astype(BF16).astype(F32)
            codes = jnp.floor(pseudo / scale + 0.5).astype(BF16).astype(F32)
            spread[rows(b * ROWS, ROWS), :] = codes * scale
        return carry

    lax.fori_loop(0, BLOCKS // 16, quantize, 0)

    def row(ref, q):
        return ref[pl.ds(q, BLOCKS, stride=ROWS), :]

    for k in range(4):
        core_send[k * BLOCKS : (k + 1) * BLOCKS, :] = row(spread, 2 * k + 1 - core).astype(BF16)

    pl.semaphore_wait(barrier, greeted)

    swap = remote(core_send, core_recv, core_sem.at[0], core_sem.at[1], at(other=True))
    swap.start()

    loads[2].wait()
    lead_q = 2 * div(rem(z + 2, 16), 4) + core
    keep = [row(spread, 2 * k + core) for k in range(4)]

    def lead_rows(step, carry):
        for k in range(4):
            b = step * 4 + k
            columns = rows(b * QBLOCK, QBLOCK)
            turned[rows(b * ROWS, ROWS), :] = base_v[:, columns] - (
                OUTER_RATE * OUTER_MOMENTUM * OUTER_MOMENTUM
            ) * mom_v[:, columns]
        return carry

    lax.fori_loop(0, BLOCKS // 4, lead_rows, 0)
    lead_send[...] = row(turned, lead_q)

    swap.wait_recv()
    for k in range(4):
        part_sum = keep[k] + core_recv[k * BLOCKS : (k + 1) * BLOCKS, :].astype(F32)
        far_send[k * BLOCKS : (k + 1) * BLOCKS, :] = part_sum.astype(BF16)
    fars = []
    for j, dz in enumerate((6, -6, 2, -2)):
        k = div(rem(z + dz + 16, 16), 4)
        fars.append(
            remote(
                far_send.at[rows(k * BLOCKS, BLOCKS)],
                far_recv.at[pl.ds(j * BLOCKS, BLOCKS)],
                far_ssem.at[j],
                far_rsem.at[j],
                at(dz),
            )
        )
        fars[-1].start()
    lead = remote(lead_send, lead_recv, lead_sem.at[0], lead_sem.at[1], at(2))
    lead.start()

    def order(j, carry):
        late = jnp.where(j >= 6, 1, 0)
        other = late * (j - 6) + (1 - late) * div(j, 3)
        turn = late * 2 + (1 - late) * rem(j * j, 3) * (1 + 2 * jnp.where(rem(j, 3) == 2, 1, 0))
        there_hi = z_hi + turn
        there_core = rem(core + other, 2)
        line = lax.broadcasted_iota(jnp.int32, (128, QBLOCK), 0)
        slot = line % SLOTS
        step = (z_lo + 2 - (slot // 4) % 4 + 4) % 4
        sign = 1 - 2 * ((slot % 4 + slot // 16) % 2)
        dz = jnp.where(step == 2, 2 * sign, jnp.where(step == 3, -1, step))
        source = (4 * there_hi + z_lo - dz + 32) % 16
        target = 8 * slot + 2 * (source // 4) + there_core
        lane = lax.broadcasted_iota(jnp.int32, (128, QBLOCK), 1)
        for half in range(2):
            wanted = jnp.where(line // SLOTS == half, target, -1)
            for n in range(4):
                hit = jnp.where(wanted == lane + n * QBLOCK, 1.0, 0.0).astype(BF16)
                first = half * 512 + n * QBLOCK
                perm[rows(j * 128, 128), first : first + QBLOCK] = hit
        return carry

    lax.fori_loop(0, 8, order, 0)

    for far in fars:
        far.wait_recv()
    lead.wait_recv()
    total = jnp.zeros((BLOCKS, QBLOCK), F32)
    for j in range(4):
        total += far_recv[j * BLOCKS : (j + 1) * BLOCKS, :].astype(F32)
    grad = total * 0.125
    gain = OUTER_RATE * (1.0 + OUTER_MOMENTUM)
    new_row = (lead_recv[...] - gain * grad).astype(BF16)
    own_class = rem(z + 2, 4)

    def place(half, slot):
        return rows((half * SLOTS + slot) * HALF, HALF)

    own_slot = 16 * y + 4 * own_class + x
    pieces[place(0, own_slot), :] = new_row[:HALF]
    pieces[place(1, own_slot), :] = new_row[HALF:]

    def first_path(kind, py, px):
        return rem(rem(px + py + kind, 4), 3)

    def choose(path, options):
        return tuple(
            jnp.where(path == 0, a, jnp.where(path == 1, b, c)) for a, b, c in zip(*options)
        )

    def send_piece(half, slot, to, sem):
        spot = pieces.at[place(half, slot)]
        remote(spot, spot, piece_ssem, sem, to).start()

    steps = [(a, b) for a in range(4) for b in range(4)]
    length = [0, 1, 2, 1]
    steps.sort(key=lambda s: length[s[0]] + length[s[1]])
    for a, b in steps[1:]:
        dz = (0, 1, 2 * mine, -1)[b]
        options = (at(dz, 0, a), at(dz, a, 0), at(0, a, b))
        for half in range(2):
            path = rem(first_path(own_class, y, x) + half, 3)
            send_piece(half, own_slot, choose(path, options), piece_rsem.at[half * SLOTS + own_slot])
    og_own[...] = grad.astype(BF16)

    third = (
        (at(0, 2), at(0, 1), at(0, 3)),
        (at(0, 0, 2), at(0, 0, 1), at(0, 0, 3)),
        (at(1), at(-1)),
    )
    at_2, at_m2 = at(2), at(-2)

    for a, b in steps:
        for path in range(3):
            px = x if path == 1 else rem(x + (a if path == 0 else b), 4)
            py = y if path == 0 else rem(y + a, 4)
            there = parity(px, py)
            dz = 0 if path == 2 else (0, -1, -2 * there, 1)[b]
            kind = rem(z + dz + 16 + 2, 4)
            slot = 16 * py + 4 * kind + px
            half = rem(path + 3 - first_path(kind, py, px), 3)

            @pl.when(half < 2)
            def _(path=path, half=half, slot=slot, there=there, own=not (a or b)):
                if not own:
                    spot = pieces.at[place(half, slot)]
                    remote(spot, spot, piece_ssem, piece_rsem.at[half * SLOTS + slot], at(2)).wait_recv()
                ends = third[path]
                if path == 2:
                    far_end = tuple(jnp.where(there == 1, p, m) for p, m in zip(at_2, at_m2))
                    ends = (far_end, *ends)
                for end, sem in zip(ends, (far_sem, near_sem, near_sem)):
                    send_piece(half, slot, end, sem)

    ogs = []
    for j, dz in enumerate((6, -6, 2, -2)):
        ogs.append(
            remote(og_own, og_recv.at[rows(z_hi * BLOCKS, BLOCKS)], og_ssem.at[j], og_rsem.at[z_hi], at(dz))
        )
        ogs[-1].start()

    loads[3].wait()
    def wait_pieces(count, sem):
        spots = pieces.at[pl.ds(0, count * HALF)]
        remote(spots, spots, piece_ssem, sem, at(2)).wait_recv()

    wait_pieces(64, near_sem)
    wait_pieces(32, far_sem)

    for half in range(2):
        for slot in range(0, SLOTS, 16):
            group = pieces[pl.ds((half * SLOTS + slot) * HALF, 16 * HALF), :]
            group = jnp.transpose(group.reshape(16, HALF, QBLOCK), (1, 0, 2))
            for b in range(HALF):
                first = (half * HALF + b) * QBLOCK
                weight[slot : slot + 16, first : first + QBLOCK] = group[b]
    keys = lax.dot_general(
        x_v[...], weight[...], (((1,), (1,)), ((), ())), preferred_element_type=F32
    ).astype(BF16)
    part[:, 0:QBLOCK] = jnp.concatenate([keys[:PACKED], keys[PACKED:]], axis=1)

    def spot(j):
        return part.at[:, pl.ds(j * QBLOCK, QBLOCK)]

    sends = []

    def send_keys(j, to_j, to):
        copy = remote(spot(j), spot(to_j), key_ssem.at[len(sends)], key_rsem.at[to_j], to)
        copy.start()
        sends.append(copy)

    def wait_keys(j):
        remote(spot(0), spot(j), key_ssem.at[0], key_rsem.at[j], at(2)).wait_recv()

    send_keys(0, 6, at(8))
    send_keys(0, 2, at(4))
    send_keys(0, 1, at(-4))
    send_keys(0, 3, at(other=True))

    for k in range(4):
        home = og_recv.at[pl.ds(k * BLOCKS, BLOCKS)]
        remote(home, home, og_ssem.at[0], og_rsem.at[k], at(2)).wait_recv()
    relay = remote(og_recv, og_other, ogc_sem.at[0], ogc_sem.at[1], at(other=True))
    relay.start()
    relay.wait_recv()
    for k in range(4):
        span = slice(k * BLOCKS, (k + 1) * BLOCKS)
        spread[pl.ds(2 * k + core, BLOCKS, stride=ROWS), :] = og_recv[span, :].astype(F32)
        spread[pl.ds(2 * k + 1 - core, BLOCKS, stride=ROWS), :] = og_other[span, :].astype(F32)

    def outer(step, carry):
        for k in range(4):
            b = step * 4 + k
            columns = rows(b * QBLOCK, QBLOCK)
            og = spread[rows(b * ROWS, ROWS), :]
            new_momentum = OUTER_MOMENTUM * mom_v[:, columns] + og
            nb_out[:, columns] = base_v[:, columns] - OUTER_RATE * (og + OUTER_MOMENTUM * new_momentum)
            nm_out[:, columns] = new_momentum
        return carry

    lax.fori_loop(0, BLOCKS // 4, outer, 0)
    for j in (1, 2):
        wait_keys(j)
        send_keys(j, j + 3, at(other=True))
    for j in (3, 4, 5):
        wait_keys(j)

    def ordered(first, last):
        held = part[:, first * QBLOCK : last * QBLOCK]
        table = perm[first * QBLOCK : last * QBLOCK, :]
        return jnp.dot(held, table, preferred_element_type=F32)

    early = ordered(0, 6)
    wait_keys(6)
    send_keys(6, 7, at(other=True))
    early += ordered(6, 7)
    wait_keys(7)
    done = (early + ordered(7, 8)).astype(BF16)
    keys_out[:PACKED, :] = done[:, :512]
    keys_out[PACKED:, :] = done[:, 512:]

    swap.wait_send()
    lead.wait_send()
    relay.wait_send()
    for copy in fars + ogs + sends:
        copy.wait_send()
    sent = pieces.at[pl.ds(0, (30 + 96) * HALF)]
    remote(sent, sent, piece_ssem, piece_rsem.at[0], at(2)).wait_send()


def store(nb, nm, keys, nb_out, nm_out, keys_out, sem):
    copies = [
        pltpu.make_async_copy(here, there, sem.at[j])
        for j, (here, there) in enumerate(((keys, keys_out), (nb, nb_out), (nm, nm_out)))
    ]
    for copy in copies:
        copy.start()
    for copy in copies:
        copy.wait()


def shards(inputs, local_weights, global_base, momentum):
    width = global_base.shape[1]
    shape = jax.ShapeDtypeStruct
    dma = pltpu.SemaphoreType.DMA
    inputs, local_weights, global_base, momentum = (
        pltpu.with_memory_space_constraint(a, pltpu.HBM)
        for a in (inputs, local_weights.reshape(ROWS, width), global_base, momentum)
    )
    results = pl.pallas_call(
        kernel,
        name="outer_step_and_keys",
        out_shape=(
            pltpu.VMEM((ROWS, width), F32),
            pltpu.VMEM((ROWS, width), F32),
            pltpu.VMEM((TOKENS, 512), BF16),
        ),
        in_specs=[pl.BlockSpec(memory_space=pl.ANY)] * 4,
        out_specs=[pl.BlockSpec(memory_space=pltpu.VMEM)] * 3,
        scratch_shapes=[
            pltpu.VMEM((ROWS, width), F32),
            pltpu.VMEM((ROWS, width), F32),
            pltpu.VMEM((ROWS, width), F32),
            pltpu.VMEM((TOKENS, width), BF16),
            pltpu.VMEM((BLOCKS * ROWS, QBLOCK), F32),
            pltpu.VMEM((4 * BLOCKS, QBLOCK), BF16),
            pltpu.VMEM((4 * BLOCKS, QBLOCK), BF16),
            pltpu.VMEM((4 * BLOCKS, QBLOCK), BF16),
            pltpu.VMEM((4 * BLOCKS, QBLOCK), BF16),
            pltpu.VMEM((BLOCKS, QBLOCK), F32),
            pltpu.VMEM((BLOCKS, QBLOCK), F32),
            pltpu.VMEM((SLOTS * BLOCKS, QBLOCK), BF16),
            pltpu.VMEM((BLOCKS * ROWS, QBLOCK), F32),
            pltpu.VMEM((SLOTS, width), BF16),
            pltpu.VMEM((BLOCKS, QBLOCK), BF16),
            pltpu.VMEM((4 * BLOCKS, QBLOCK), BF16),
            pltpu.VMEM((4 * BLOCKS, QBLOCK), BF16),
            pltpu.VMEM((PACKED, 8 * QBLOCK), BF16),
            pltpu.VMEM((8 * QBLOCK, 1024), BF16),
            dma((4,)),
            dma((2,)),
            dma((4,)),
            dma((4,)),
            dma((2,)),
            dma,
            dma((2 * SLOTS,)),
            dma,
            dma,
            dma((4,)),
            dma((4,)),
            dma((2,)),
            dma((7,)),
            dma((8,)),
        ],
        compiler_params=pltpu.CompilerParams(
            collective_id=0, has_side_effects=True, vmem_limit_bytes=40 * 2**20
        ),
        cost_estimate=pl.CostEstimate(flops=2 * 192 * 64 * 8192, bytes_accessed=5 * 2**20, transcendentals=1024),
    )(inputs, local_weights, global_base, momentum)
    results = [pltpu.with_memory_space_constraint(a, pltpu.VMEM) for a in results]
    return pl.pallas_call(
        store,
        name="store_results",
        out_shape=tuple(shape(a.shape, a.dtype) for a in results),
        in_specs=[pl.BlockSpec(memory_space=pltpu.VMEM)] * 3,
        out_specs=[pl.BlockSpec(memory_space=pltpu.HBM)] * 3,
        scratch_shapes=[dma((3,))],
        compiler_params=pltpu.CompilerParams(vmem_limit_bytes=2 * 2**20),
    )(*results)


def solution(mesh):
    return jax.shard_map(
        shards,
        mesh=mesh,
        in_specs=(P("fsdp", None), P("replica", "fsdp", None), P("fsdp", None), P("fsdp", None)),
        out_specs=(P("fsdp", None), P("fsdp", None), P("fsdp", None)),
        check_vma=False,
    )
```
